32 devices in a mesh: grp: 4 (over y, x), seq: 8 (over z, core).
Axes of the slice: x: 2, y: 2, z: 4, core: 2. Of those that a mesh axis runs over, the one named last changes fastest.
Arguments:
- tiles: bfloat16 [8, 4096, 768], P('grp', 'seq'), may hold values from -8 to 8
- counts: int32 [8], P('grp'), may hold values from 1024 to 4096, as said below
- ln1_gain: float32 [768], replicated, may hold values from 0.1 to 1.9
- qkv_weight: bfloat16 [768, 2304], replicated, may hold values from -0.18042196 to 0.18042196
- out_weight: bfloat16 [768, 768], replicated, may hold values from -0.21875 to 0.21875
- ln2_gain: float32 [768], replicated, may hold values from 0.1 to 1.9
- ff_in: bfloat16 [768, 3072], replicated, may hold values from -0.21875 to 0.21875
- ff_out: bfloat16 [3072, 768], replicated, may hold values from -0.109375 to 0.109375
- pool_weight: bfloat16 [768, 768], P('grp'), may hold values from -0.18042196 to 0.18042196
- class_weight: float32 [384, 8], replicated, may hold values from -3 to 6
Outputs:
- encoded: bfloat16 [8, 4096, 768], P('grp', 'seq')
- pooled: float32 [8, 8, 768], P('grp')
The draws below stay inside these ranges and needn't reach their ends.
Inputs may be any that keep to these rules, and one draw needn't show every extreme that they name: The valid tiles of a slide are its first counts tiles in scan order; some slide has all 4096 tiles valid.
All inputs are finite; a program needn't handle non-finite values.
Results may differ from the reference program's by a relative error of at most 0.015.
Values may be sent and summed in bfloat16 or wider, within the bound.
A program may use at most 128 MiB of HBM per device.

```python
import jax
import jax.numpy as jnp
from jax import lax

D = 768
HEADS = 16
FF = 3072
ATT_H = 384
CLASSES = 8
BLOCK = 256
SLIDES = 8
TILES = 4096
N_SEQ = 8


def draw_counts(key, part):
    values = jax.random.randint(jax.random.fold_in(key, 11), (SLIDES,), TILES // 4, TILES + 1)
    chosen = jax.random.randint(jax.random.fold_in(key, 17), (), 0, SLIDES)
    return jnp.where(jnp.arange(SLIDES) == chosen, TILES, values).astype(jnp.int32)


def draw_tiles(key, part):
    shape = (SLIDES, TILES, D)
    values = jax.random.truncated_normal(jax.random.fold_in(key, 21), -6.0, 6.0, shape, jnp.float32)
    return values.astype(jnp.bfloat16)


def draw_qkv_weight(key, part):
    shape = (D, 3 * D)
    values = jax.random.truncated_normal(jax.random.fold_in(key, 31), -4.0, 4.0, shape, jnp.float32) * D ** (-0.5)
    return values.astype(jnp.bfloat16)


def draw_pool_weight(key, part):
    shape = (D, 2 * ATT_H)
    values = jax.random.truncated_normal(jax.random.fold_in(key, 41), -4.0, 4.0, shape, jnp.float32) * D ** (-0.5)
    return values.astype(jnp.bfloat16)


def draw_class_weight(key, part):
    shape = (ATT_H, CLASSES)
    values = jax.random.truncated_normal(jax.random.fold_in(key, 51), -6.0, 6.0, shape, jnp.float32) * 0.5
    return values.astype(jnp.float32)


def noise(rng, dims, deviation, most, kind=jnp.bfloat16):
    entries = jax.random.normal(rng, dims, jnp.float32) * deviation
    return jnp.minimum(jnp.maximum(entries, -most), most).astype(kind)


def setup_inputs(seed: int = 0) -> dict:
    splits = jax.random.split(jax.random.key(seed), 11)
    return {
        "tiles": draw_tiles(jax.random.fold_in(splits[10], 71), 0),
        "counts": draw_counts(jax.random.fold_in(splits[10], 71), 0),
        "ln1_gain": jnp.clip(1.0 + 0.18 * jax.random.normal(splits[2], (D,), jnp.float32), 0.1, 1.9),
        "qkv_weight": draw_qkv_weight(jax.random.fold_in(splits[10], 71), 0),
        "out_weight": noise(splits[4], (D, D), D ** -0.5, 0.21875),
        "ln2_gain": jnp.clip(1.0 + 0.18 * jax.random.normal(splits[5], (D,), jnp.float32), 0.1, 1.9),
        "ff_in": noise(splits[6], (D, FF), D ** -0.5, 0.21875),
        "ff_out": noise(splits[7], (FF, D), FF ** -0.5, 0.109375),
        "pool_weight": draw_pool_weight(jax.random.fold_in(splits[10], 71), 0),
        "class_weight": draw_class_weight(jax.random.fold_in(splits[10], 71), 0),
    }


def normalize(values, gain):
    xf = values.astype(jnp.float32)
    centre = lax.optimization_barrier(jnp.mean(xf, axis=-1, keepdims=True))
    spread = lax.optimization_barrier(jnp.mean((xf - centre) ** 2, axis=-1, keepdims=True))
    return (xf - centre) * lax.rsqrt(spread + 1e-05) * gain

def attend(query, key_rows, value_rows, keep):
    scale = 1.0 / query.shape[-1] ** 0.5
    scores = jnp.einsum('qhd,khd->hqk', query.astype(jnp.float32), key_rows.astype(jnp.float32)) * scale
    scores = jnp.where(keep[None, None, :], scores, -1e+30)
    peak = lax.optimization_barrier(jnp.max(scores, axis=-1))
    probs = jnp.exp(scores - peak[..., None])
    total = lax.optimization_barrier(jnp.sum(probs, axis=-1))
    weights = probs.astype(jnp.bfloat16).astype(jnp.float32)
    result = jnp.einsum('hqk,khd->qhd', weights, value_rows.astype(jnp.float32)) / total.T[..., None]
    return (result, (peak + jnp.log(total)).T)

def one_slide(args):
    tiles, count, ln1_gain, qkv_weight, out_weight, ln2_gain, ff_in, ff_out, pool_weight, class_weight = args
    rows = tiles.shape[0]
    width = tiles.shape[1]
    head_dim = width // HEADS
    valid = jnp.arange(rows, dtype=jnp.int32) < count
    normed = normalize(tiles, ln1_gain).astype(jnp.bfloat16)
    proj = jnp.dot(normed, qkv_weight, preferred_element_type=jnp.float32).astype(jnp.bfloat16)
    query = proj[:, :width].reshape(rows, HEADS, head_dim)
    key_rows = proj[:, width:2 * width].reshape(rows, HEADS, head_dim)
    value_rows = proj[:, 2 * width:].reshape(rows, HEADS, head_dim)
    nblocks = rows // BLOCK

    def near(item):
        return attend(item[0], item[1], item[2], item[3])
    near_out, near_lse = lax.map(near, (query.reshape(nblocks, BLOCK, HEADS, head_dim), key_rows.reshape(nblocks, BLOCK, HEADS, head_dim), value_rows.reshape(nblocks, BLOCK, HEADS, head_dim), valid.reshape(nblocks, BLOCK)))
    near_out = near_out.reshape(rows, HEADS, head_dim)
    near_lse = near_lse.reshape(rows, HEADS)
    rate = N_SEQ
    per_class = rows // rate

    def regroup(arr):
        return jnp.swapaxes(arr.reshape((per_class, rate) + arr.shape[1:]), 0, 1)
    far_out, far_lse = lax.map(near, (regroup(query), regroup(key_rows), regroup(value_rows), regroup(valid)))
    far_out = jnp.swapaxes(far_out, 0, 1).reshape(rows, HEADS, head_dim)
    far_lse = jnp.swapaxes(far_lse, 0, 1).reshape(rows, HEADS)
    far_out = lax.optimization_barrier(far_out.astype(jnp.bfloat16)).astype(jnp.float32)
    top = jnp.maximum(near_lse, far_lse)
    near_w = jnp.exp(near_lse - top)
    far_w = jnp.exp(far_lse - top)
    mixed = (near_w[..., None] * near_out + far_w[..., None] * far_out) / (near_w + far_w)[..., None]
    mixed = mixed.reshape(rows, width).astype(jnp.bfloat16)
    resid = tiles.astype(jnp.float32) + jnp.dot(mixed, out_weight, preferred_element_type=jnp.float32)
    normed2 = normalize(resid, ln2_gain).astype(jnp.bfloat16)
    act = jax.nn.gelu(jnp.dot(normed2, ff_in, preferred_element_type=jnp.float32), approximate=False).astype(jnp.bfloat16)
    encoded = (resid + jnp.dot(act, ff_out, preferred_element_type=jnp.float32)).astype(jnp.bfloat16)
    encoded = jnp.where(valid[:, None], encoded, jnp.zeros_like(encoded))
    zed = jnp.dot(encoded, pool_weight, preferred_element_type=jnp.float32)
    hidden = pool_weight.shape[1] // 2
    gate = jnp.tanh(zed[:, :hidden]) * jax.nn.sigmoid(zed[:, hidden:])
    logits = jnp.dot(gate, class_weight, precision=lax.Precision.HIGHEST)
    logits = jnp.where(valid[:, None], logits, -1e+30)
    peak = lax.optimization_barrier(jnp.max(logits, axis=0))
    expo = jnp.exp(logits - peak[None, :]) * valid[:, None].astype(jnp.float32)
    numer = jnp.dot(expo.T, encoded.astype(jnp.float32), precision=lax.Precision.HIGHEST)
    pooled = numer / lax.optimization_barrier(jnp.sum(expo, axis=0))[:, None]
    return (encoded, pooled)

def reference(tiles, counts, ln1_gain, qkv_weight, out_weight, ln2_gain, ff_in, ff_out, pool_weight, class_weight):

    def run(item):
        return one_slide((item[0], item[1], ln1_gain, qkv_weight, out_weight, ln2_gain, ff_in, ff_out, pool_weight, class_weight))
    encoded, pooled = lax.map(run, (tiles, counts))
    return (encoded, pooled)
```

```python
import functools
import math

import jax
import jax.numpy as jnp
from jax import lax
from jax.experimental import pallas as pl
from jax.experimental.pallas import tpu as pltpu
from jax.sharding import PartitionSpec as P

HEADS = 16
BLOCK = 256
AUG = 16
NEG = -1e30
NT = (((1,), (1,)), ((), ()))
TN = (((0,), (0,)), ((), ()))


def normalize(xf, gain):
    centre = jnp.mean(xf, axis=-1, keepdims=True)
    spread = jnp.mean((xf - centre) ** 2, axis=-1, keepdims=True)
    return (xf - centre) * lax.rsqrt(spread + 1e-05) * gain


def spread_matrix(rows, ratio):
    chunk = rows // ratio
    r = lax.broadcasted_iota(jnp.int32, (rows, rows), 0)
    t = lax.broadcasted_iota(jnp.int32, (rows, rows), 1)
    return jnp.where((r % chunk) * ratio + r // chunk == t, 1.0, 0.0)


def attend(kt, qt, vt, head_dim):
    scale = 1.0 / head_dim**0.5
    c = scale * math.log2(math.e)
    s = lax.dot_general(kt, qt, TN, preferred_element_type=jnp.float32)
    m = jnp.max(s, axis=0, keepdims=True)
    p = jnp.exp2((s - m) * c).astype(jnp.bfloat16)
    o = jnp.dot(vt, p, preferred_element_type=jnp.float32)
    total = o[head_dim : head_dim + 1]
    return o[:head_dim] / total, m * scale + jnp.log(total)


def attention_kernel(
    ratio,
    counts_ref,
    tiles_ref,
    gain_ref,
    w_ref,
    mixed_ref,
    wt,
    spread_ref,
    x_near,
    x_send,
    x_recv,
    proj,
    near_out,
    near_lse,
    o_t,
    l_t,
    o_send,
    o_recv,
    l_send,
    l_recv,
    l_rows,
    x_ss,
    x_rs,
    o_ss,
    o_rs,
    l_ss,
    l_rs,
):
    me = lax.axis_index("seq")
    slides, rows, width = tiles_ref.shape
    head_dim = width // HEADS
    nblocks = rows // BLOCK
    chunk = rows // ratio

    def x_copy(s, peer):
        return pltpu.make_async_remote_copy(
            src_ref=x_send.at[s, peer],
            dst_ref=x_recv.at[s, me],
            send_sem=x_ss.at[s, peer],
            recv_sem=x_rs.at[s, me],
            device_id={"seq": peer},
            device_id_type=pl.DeviceIdType.MESH,
        )

    def x_arrival(s, peer):
        return pltpu.make_async_remote_copy(
            src_ref=x_send.at[s, peer],
            dst_ref=x_recv.at[s, peer],
            send_sem=x_ss.at[s, peer],
            recv_sem=x_rs.at[s, peer],
            device_id={"seq": peer},
            device_id_type=pl.DeviceIdType.MESH,
        )

    def o_copy(s, peer, slot):
        return pltpu.make_async_remote_copy(
            src_ref=o_send.at[s, peer],
            dst_ref=o_recv.at[s, slot],
            send_sem=o_ss.at[s, peer],
            recv_sem=o_rs.at[s, slot],
            device_id={"seq": peer},
            device_id_type=pl.DeviceIdType.MESH,
        )

    def l_copy(s, peer, slot):
        return pltpu.make_async_remote_copy(
            src_ref=l_send.at[s, peer],
            dst_ref=l_recv.at[s, slot],
            send_sem=l_ss.at[s, peer],
            recv_sem=l_rs.at[s, slot],
            device_id={"seq": peer},
            device_id_type=pl.DeviceIdType.MESH,
        )

    def partner(k):
        return lax.rem(me + k, ratio)

    barrier = pltpu.get_barrier_semaphore()
    for k in range(1, ratio):
        pl.semaphore_signal(
            barrier, inc=1, device_id={"seq": partner(k)}, device_id_type=pl.DeviceIdType.MESH
        )

    spread_ref[...] = spread_matrix(rows, ratio).astype(jnp.bfloat16)
    for s in range(slides):
        xf = tiles_ref[s].astype(jnp.float32)
        normed = normalize(xf, gain_ref[...]).astype(jnp.bfloat16)
        x_near[s] = normed
        moved = jnp.dot(spread_ref[...], normed, preferred_element_type=jnp.float32)
        x_send[s] = moved.astype(jnp.bfloat16).reshape(ratio, chunk, width)
        if s == 0:
            pl.semaphore_wait(barrier, ratio - 1)

        def send(k, carry, s=s):
            x_copy(s, partner(k)).start()
            return carry

        lax.fori_loop(1, ratio, send, 0)

    for j in range(3):
        wt[j] = w_ref[:, j * width : (j + 1) * width].T
    first = lax.broadcasted_iota(jnp.int32, (AUG, rows), 0) == 0
    lane = lax.broadcasted_iota(jnp.int32, (AUG, rows), 1)
    ones = jnp.where(first, 1.0, 0.0).astype(jnp.bfloat16)
    for h in range(HEADS):
        proj[0, h, head_dim:, :] = ones
        proj[2, h, head_dim:, :] = ones

    def project(x, keep):
        bias = jnp.where(first & jnp.logical_not(keep), NEG, 0.0).astype(jnp.bfloat16)
        for h in range(HEADS):
            proj[1, h, head_dim:, :] = bias

        def part(j, carry):
            y = lax.dot_general(wt[j], x, NT, preferred_element_type=jnp.float32)
            proj[j, :, :head_dim, :] = y.astype(jnp.bfloat16).reshape(HEADS, head_dim, rows)
            return carry

        lax.fori_loop(0, 3, part, 0)

    local_pos = me * rows + lane

    def near(s, carry):
        project(x_near[s], local_pos < counts_ref[s])

        def head(h, carry):
            for b in range(nblocks):
                cols = slice(b * BLOCK, (b + 1) * BLOCK)
                out, lse = attend(
                    proj[1, h, :, cols], proj[0, h, :, cols], proj[2, h, :, cols], head_dim
                )
                near_out[s, h, :, cols] = out
                near_lse[s, h, :, cols] = lse
            return carry

        lax.fori_loop(0, HEADS, head, 0, unroll=4)
        return carry

    lax.fori_loop(0, slides, near, 0)

    class_pos = lane * ratio + me

    def far(s, carry):
        def arrive(k, carry):
            x_arrival(s, partner(k)).wait_recv()
            return carry

        lax.fori_loop(1, ratio, arrive, 0)
        x_recv[s, me] = x_send[s, me]
        project(x_recv[s].reshape(rows, width), class_pos < counts_ref[s])

        def head(h, carry):
            out, lse = attend(proj[1, h], proj[0, h], proj[2, h], head_dim)
            o_t[h] = out.astype(jnp.bfloat16)
            l_t[h] = lse
            return carry

        lax.fori_loop(0, HEADS, head, 0, unroll=2)
        o_send[s] = o_t[...].reshape(width, rows).T.reshape(ratio, chunk, width)
        lse = l_t[...].reshape(HEADS, rows)
        for d in range(ratio):
            l_send[s, d] = lse[:, d * chunk : (d + 1) * chunk]

        def send(k, carry):
            o_copy(s, partner(k), me).start()
            l_copy(s, partner(k), me).start()
            return carry

        lax.fori_loop(1, ratio, send, 0)
        return carry

    lax.fori_loop(0, slides, far, 0)

    def mix(s, carry):
        def arrive(k, carry):
            o_copy(s, partner(k), partner(k)).wait_recv()
            l_copy(s, partner(k), partner(k)).wait_recv()
            return carry

        lax.fori_loop(1, ratio, arrive, 0)
        o_recv[s, me] = o_send[s, me]
        l_recv[s, me] = l_send[s, me]
        for c in range(ratio):
            l_rows[c] = l_recv[s, c].T
        far_lse = jnp.dot(
            l_rows[...].reshape(rows, HEADS).T,
            spread_ref[...].astype(jnp.float32),
            precision=lax.Precision.HIGHEST,
            preferred_element_type=jnp.float32,
        ).reshape(HEADS, 1, rows)
        n_lse = near_lse[s]
        top = jnp.maximum(n_lse, far_lse)
        n_w = jnp.exp(n_lse - top)
        f_w = jnp.exp(far_lse - top)
        inv = 1.0 / (n_w + f_w)
        n_w = n_w * inv
        f_w = f_w * inv
        far_out = lax.dot_general(
            o_recv[s].reshape(rows, width),
            spread_ref[...],
            TN,
            preferred_element_type=jnp.float32,
        ).reshape(HEADS, head_dim, rows)
        mixed = (n_w * near_out[s] + f_w * far_out).astype(jnp.bfloat16)
        mixed_ref[s] = mixed.reshape(width, rows).T
        return carry

    lax.fori_loop(0, slides, mix, 0)

    def drain(i, carry):
        s = i // (ratio - 1)
        peer = partner(i % (ratio - 1) + 1)
        x_copy(s, peer).wait_send()
        o_copy(s, peer, me).wait_send()
        l_copy(s, peer, me).wait_send()
        return carry

    lax.fori_loop(0, slides * (ratio - 1), drain, 0)


def attention(tiles, counts, gain, qkv_weight, ratio):
    slides, rows, width = tiles.shape
    head_dim = width // HEADS
    chunk = rows // ratio
    bf16, f32 = jnp.bfloat16, jnp.float32
    vmem = pl.BlockSpec(memory_space=pltpu.VMEM)
    sem = pltpu.SemaphoreType.DMA((slides, ratio))
    return pl.pallas_call(
        functools.partial(attention_kernel, ratio),
        out_shape=jax.ShapeDtypeStruct((slides, rows, width), bf16),
        in_specs=[pl.BlockSpec(memory_space=pltpu.SMEM), vmem, vmem, vmem],
        out_specs=vmem,
        scratch_shapes=[
            pltpu.VMEM((3, width, width), bf16),
            pltpu.VMEM((rows, rows), bf16),
            pltpu.VMEM((slides, rows, width), bf16),
            pltpu.VMEM((slides, ratio, chunk, width), bf16),
            pltpu.VMEM((slides, ratio, chunk, width), bf16),
            pltpu.VMEM((3, HEADS, head_dim + AUG, rows), bf16),
            pltpu.VMEM((slides, HEADS, head_dim, rows), f32),
            pltpu.VMEM((slides, HEADS, 1, rows), f32),
            pltpu.VMEM((HEADS, head_dim, rows), bf16),
            pltpu.VMEM((HEADS, 1, rows), f32),
            pltpu.VMEM((slides, ratio, chunk, width), bf16),
            pltpu.VMEM((slides, ratio, chunk, width), bf16),
            pltpu.VMEM((slides, ratio, HEADS, chunk), f32),
            pltpu.VMEM((slides, ratio, HEADS, chunk), f32),
            pltpu.VMEM((ratio, chunk, HEADS), f32),
            sem,
            sem,
            sem,
            sem,
            sem,
            sem,
        ],
        compiler_params=pltpu.CompilerParams(
            collective_id=0, has_side_effects=True, vmem_limit_bytes=48 * 2**20
        ),
        cost_estimate=pl.CostEstimate(
            flops=2 * slides * rows * width * width * 8,
            bytes_accessed=8 * slides * rows * width,
            transcendentals=0,
        ),
    )(counts, tiles, gain.reshape(1, width), qkv_weight)


def gelu(x):
    return 0.5 * x * (1.0 + lax.erf(x * math.sqrt(0.5)))


def feed_kernel(
    counts_ref,
    tiles_ref,
    mixed_ref,
    wo_ref,
    gain_ref,
    fi_ref,
    fo_ref,
    pw_ref,
    cw_ref,
    enc_ref,
    stat_ref,
    peak_s,
    total_s,
    numer_s,
):
    s = pl.program_id(0)
    t = pl.program_id(1)
    here = lax.axis_index("seq")
    size, width = mixed_ref.shape[1:]
    f32, bf16 = jnp.float32, jnp.bfloat16
    start = here * size * pl.num_programs(1) + t * size
    count = counts_ref[s]
    resid = tiles_ref[0].astype(f32) + jnp.dot(
        mixed_ref[0], wo_ref[...], preferred_element_type=f32
    )
    normed = normalize(resid, gain_ref[...]).astype(bf16)
    ff = fi_ref.shape[1]
    step = width
    out = resid
    for j in range(0, ff, step):
        h = jnp.dot(normed, fi_ref[:, j : j + step], preferred_element_type=f32)
        act = gelu(h).astype(bf16)
        out = out + jnp.dot(act, fo_ref[j : j + step, :], preferred_element_type=f32)
    rowpos = start + lax.broadcasted_iota(jnp.int32, (size, width), 0)
    encoded = jnp.where(rowpos < count, out, 0.0).astype(bf16)
    enc_ref[0] = encoded
    zed = jnp.dot(encoded, pw_ref[...], preferred_element_type=f32)
    hidden = zed.shape[1] // 2
    gate = jnp.tanh(zed[:, :hidden]) * jax.nn.sigmoid(zed[:, hidden:])
    logits = lax.dot_general(
        cw_ref[...], gate, NT, precision=lax.Precision.HIGHEST, preferred_element_type=f32
    )
    classes = logits.shape[0]
    keep = start + lax.broadcasted_iota(jnp.int32, (classes, size), 1) < count
    logits = jnp.where(keep, logits, NEG)

    @pl.when(t == 0)
    def _():
        peak_s[...] = jnp.full_like(peak_s, NEG)
        total_s[...] = jnp.zeros_like(total_s)
        numer_s[...] = jnp.zeros_like(numer_s)

    old = peak_s[:, :1]
    peak = jnp.maximum(old, jnp.max(logits, axis=1, keepdims=True))
    fade = jnp.exp(old - peak)
    expo = jnp.where(keep, jnp.exp(logits - peak), 0.0)
    numer = jnp.dot(
        expo, encoded.astype(f32), precision=lax.Precision.HIGHEST, preferred_element_type=f32
    )
    total_s[...] = total_s[...] * fade + jnp.sum(expo, axis=1, keepdims=True)
    numer_s[...] = numer_s[...] * fade + numer
    peak_s[...] = jnp.broadcast_to(peak, peak_s.shape)

    @pl.when(t == pl.num_programs(1) - 1)
    def _():
        stat_ref[0, :, :width] = numer_s[...]
        stat_ref[0, :, width : width + 128] = total_s[...]
        stat_ref[0, :, width + 128 :] = peak_s[...]


def feed(counts, tiles, mixed, wo, gain, fi, fo, pw, cw):
    slides, rows, width = tiles.shape
    size = min(512, rows)
    classes = cw.shape[0]
    f32 = jnp.float32

    def whole(a):
        return pl.BlockSpec(a.shape, lambda s, t: (0, 0))

    gain = gain.reshape(1, width)
    block = pl.BlockSpec((1, size, width), lambda s, t: (s, t, 0))
    return pl.pallas_call(
        feed_kernel,
        grid=(slides, rows // size),
        out_shape=(
            jax.ShapeDtypeStruct(tiles.shape, tiles.dtype),
            jax.ShapeDtypeStruct((slides, classes, width + 256), f32),
        ),
        in_specs=[
            pl.BlockSpec(memory_space=pltpu.SMEM),
            block,
            block,
            whole(wo),
            whole(gain),
            whole(fi),
            whole(fo),
            whole(pw),
            whole(cw),
        ],
        out_specs=(block, pl.BlockSpec((1, classes, width + 256), lambda s, t: (s, 0, 0))),
        scratch_shapes=[
            pltpu.VMEM((classes, 128), f32),
            pltpu.VMEM((classes, 128), f32),
            pltpu.VMEM((classes, width), f32),
        ],
        compiler_params=pltpu.CompilerParams(vmem_limit_bytes=56 * 2**20),
        cost_estimate=pl.CostEstimate(
            flops=2 * slides * rows * width * (2 * width + 2 * fi.shape[1]),
            bytes_accessed=8 * slides * rows * width,
            transcendentals=0,
        ),
    )(counts, tiles, mixed, wo, gain, fi, fo, pw, cw)


def pool_kernel(ratio, stat_ref, out_ref, got, ss, rs):
    me = lax.axis_index("seq")
    width = out_ref.shape[-1]

    def copy(peer, slot):
        return pltpu.make_async_remote_copy(
            src_ref=stat_ref,
            dst_ref=got.at[slot],
            send_sem=ss.at[peer],
            recv_sem=rs.at[slot],
            device_id={"seq": peer},
            device_id_type=pl.DeviceIdType.MESH,
        )

    def partner(k):
        return lax.rem(me + k, ratio)

    barrier = pltpu.get_barrier_semaphore()
    for k in range(1, ratio):
        pl.semaphore_signal(
            barrier, inc=1, device_id={"seq": partner(k)}, device_id_type=pl.DeviceIdType.MESH
        )
    pl.semaphore_wait(barrier, ratio - 1)

    def send(k, carry):
        copy(partner(k), me).start()
        return carry

    lax.fori_loop(1, ratio, send, 0)
    got[me] = stat_ref[...]

    def arrive(k, carry):
        copy(partner(k), partner(k)).wait_recv()
        return carry

    lax.fori_loop(1, ratio, arrive, 0)
    peaks = got[:, :, :, width + 128 :]
    peak = jnp.max(peaks, axis=0)
    fade = jnp.exp(peaks - peak[None])
    total = jnp.sum(got[:, :, :, width : width + 128] * fade, axis=0)
    inv = 1.0 / total
    for j in range(0, width, 128):
        numer = jnp.sum(got[:, :, :, j : j + 128] * fade, axis=0)
        out_ref[:, :, j : j + 128] = numer * inv

    def drain(k, carry):
        copy(partner(k), me).wait_send()
        return carry

    lax.fori_loop(1, ratio, drain, 0)


def pool(stat, width, ratio):
    slides, classes, _ = stat.shape
    vmem = pl.BlockSpec(memory_space=pltpu.VMEM)
    return pl.pallas_call(
        functools.partial(pool_kernel, ratio),
        out_shape=jax.ShapeDtypeStruct((slides, classes, width), jnp.float32),
        in_specs=[vmem],
        out_specs=vmem,
        scratch_shapes=[
            pltpu.VMEM((ratio,) + stat.shape, jnp.float32),
            pltpu.SemaphoreType.DMA((ratio,)),
            pltpu.SemaphoreType.DMA((ratio,)),
        ],
        compiler_params=pltpu.CompilerParams(collective_id=1, has_side_effects=True),
    )(stat)


def local(
    tiles,
    counts,
    ln1_gain,
    qkv_weight,
    out_weight,
    ln2_gain,
    ff_in,
    ff_out,
    pool_weight,
    class_weight,
):
    ratio = lax.axis_size("seq")
    pw = lax.all_gather(pool_weight, "grp", axis=0, tiled=True)
    mixed = attention(tiles, counts, ln1_gain, qkv_weight, ratio)
    encoded, stat = feed(
        counts, tiles, mixed, out_weight, ln2_gain, ff_in, ff_out, pw, class_weight.T
    )
    pooled = pool(stat, tiles.shape[-1], ratio)
    return (encoded, pooled)


def solution(mesh):
    placed = (P("grp", "seq", None), P("grp"), P(), P(), P(), P(), P(), P(), P("grp", None), P())
    return jax.shard_map(
        local,
        mesh=mesh,
        in_specs=placed,
        out_specs=(P("grp", "seq", None), P("grp", None, None)),
        check_vma=False,
    )
```

```python
import functools
import math

import jax
import jax.numpy as jnp
from jax import lax
from jax.experimental import pallas as pl
from jax.experimental.pallas import tpu as pltpu
from jax.sharding import PartitionSpec as P

HEADS = 16
BLOCK = 256
AUG = 16
NEG = -1e30
NT = (((1,), (1,)), ((), ()))
TN = (((0,), (0,)), ((), ()))


def normalize(xf, gain):
    centre = jnp.mean(xf, axis=-1, keepdims=True)
    spread = jnp.mean((xf - centre) ** 2, axis=-1, keepdims=True)
    return (xf - centre) * lax.rsqrt(spread + 1e-05) * gain


def spread_matrix(rows, ratio):
    chunk = rows // ratio
    r = lax.broadcasted_iota(jnp.int32, (rows, rows), 0)
    t = lax.broadcasted_iota(jnp.int32, (rows, rows), 1)
    return jnp.where((r % chunk) * ratio + r // chunk == t, 1.0, 0.0)


def attend(kt, qt, vt, head_dim):
    scale = 1.0 / head_dim**0.5
    c = scale * math.log2(math.e)
    s = lax.dot_general(kt, qt, TN, preferred_element_type=jnp.float32)
    m = jnp.max(s, axis=0, keepdims=True)
    p = jnp.exp2((s - m) * c).astype(jnp.bfloat16)
    o = jnp.dot(vt, p, preferred_element_type=jnp.float32)
    total = o[head_dim : head_dim + 1]
    return o[:head_dim] / total, m * scale + jnp.log(total)


def gelu(x):
    return 0.5 * x * (1.0 + lax.erf(x * math.sqrt(0.5)))


def layer_kernel(
    ratio,
    counts_ref,
    tiles_hbm,
    gain_ref,
    gain2_ref,
    cw_ref,
    w_hbm,
    wo_hbm,
    fi_hbm,
    fo_hbm,
    pw_hbm,
    enc_ref,
    pooled_ref,
    tiles_ref,
    w_ref,
    wo_ref,
    fi_ref,
    fo_ref,
    pw_ref,
    wt,
    spread_ref,
    x_near,
    x_send,
    x_recv,
    proj,
    near_out,
    near_lse,
    o_t,
    l_t,
    o_send,
    o_recv,
    l_send,
    l_recv,
    l_rows,
    mixed_ref,
    stat,
    stat_recv,
    row_send,
    row_recv,
    x_ss,
    x_rs,
    o_ss,
    o_rs,
    l_ss,
    l_rs,
    s_ss,
    s_rs,
    r_ss,
    r_rs,
    t_sem,
    w_sem,
):
    me = lax.axis_index("seq")
    slides, rows, width = tiles_ref.shape
    head_dim = width // HEADS
    nblocks = rows // BLOCK
    chunk = rows // ratio
    classes = cw_ref.shape[0]
    tile_loads = [
        pltpu.make_async_copy(tiles_hbm.at[s], tiles_ref.at[s], t_sem.at[s]) for s in range(slides)
    ]
    pairs = (
        (w_hbm, w_ref),
        (wo_hbm, wo_ref),
        (fi_hbm, fi_ref),
        (fo_hbm, fo_ref),
        (pw_hbm, pw_ref),
    )
    loads = [pltpu.make_async_copy(a, b, w_sem.at[i]) for i, (a, b) in enumerate(pairs)]
    for load in tile_loads + loads:
        load.start()

    def x_copy(s, peer):
        return pltpu.make_async_remote_copy(
            src_ref=x_send.at[s, peer],
            dst_ref=x_recv.at[s, me],
            send_sem=x_ss.at[s, peer],
            recv_sem=x_rs.at[s, me],
            device_id={"seq": peer},
            device_id_type=pl.DeviceIdType.MESH,
        )

    def x_arrival(s, peer):
        return pltpu.make_async_remote_copy(
            src_ref=x_send.at[s, peer],
            dst_ref=x_recv.at[s, peer],
            send_sem=x_ss.at[s, peer],
            recv_sem=x_rs.at[s, peer],
            device_id={"seq": peer},
            device_id_type=pl.DeviceIdType.MESH,
        )

    def o_copy(s, peer, slot):
        return pltpu.make_async_remote_copy(
            src_ref=o_send.at[s, peer],
            dst_ref=o_recv.at[s, slot],
            send_sem=o_ss.at[s, peer],
            recv_sem=o_rs.at[s, slot],
            device_id={"seq": peer},
            device_id_type=pl.DeviceIdType.MESH,
        )

    def l_copy(s, peer, slot):
        return pltpu.make_async_remote_copy(
            src_ref=l_send.at[s, peer],
            dst_ref=l_recv.at[s, slot],
            send_sem=l_ss.at[s, peer],
            recv_sem=l_rs.at[s, slot],
            device_id={"seq": peer},
            device_id_type=pl.DeviceIdType.MESH,
        )

    def s_copy(s, owner, slot):
        return pltpu.make_async_remote_copy(
            src_ref=stat.at[s, owner],
            dst_ref=stat_recv.at[s, slot],
            send_sem=s_ss.at[s, owner],
            recv_sem=s_rs.at[s, slot],
            device_id={"seq": owner},
            device_id_type=pl.DeviceIdType.MESH,
        )

    def r_copy(peer, slot):
        return pltpu.make_async_remote_copy(
            src_ref=row_send,
            dst_ref=row_recv.at[slot],
            send_sem=r_ss.at[peer],
            recv_sem=r_rs.at[slot],
            device_id={"seq": peer},
            device_id_type=pl.DeviceIdType.MESH,
        )

    def partner(k):
        return lax.rem(me + k, ratio)

    barrier = pltpu.get_barrier_semaphore()
    for k in range(1, ratio):
        pl.semaphore_signal(
            barrier, inc=1, device_id={"seq": partner(k)}, device_id_type=pl.DeviceIdType.MESH
        )

    spread_ref[...] = spread_matrix(rows, ratio).astype(jnp.bfloat16)
    for s in range(slides):
        tile_loads[s].wait()
        xf = tiles_ref[s].astype(jnp.float32)
        normed = normalize(xf, gain_ref[...].reshape(1, width)).astype(jnp.bfloat16)
        x_near[s] = normed
        moved = jnp.dot(spread_ref[...], normed, preferred_element_type=jnp.float32)
        x_send[s] = moved.astype(jnp.bfloat16).reshape(ratio, chunk, width)
        if s == 0:
            pl.semaphore_wait(barrier, ratio - 1)

        def send(k, carry, s=s):
            x_copy(s, partner(k)).start()
            return carry

        lax.fori_loop(1, ratio, send, 0)

    loads[0].wait()
    for j in range(3):
        wt[j] = w_ref[:, j * width : (j + 1) * width].T
    first = lax.broadcasted_iota(jnp.int32, (AUG, rows), 0) == 0
    lane = lax.broadcasted_iota(jnp.int32, (AUG, rows), 1)
    ones = jnp.where(first, 1.0, 0.0).astype(jnp.bfloat16)
    for h in range(HEADS):
        proj[0, h, head_dim:, :] = ones
        proj[2, h, head_dim:, :] = ones

    def project(x, keep):
        bias = jnp.where(first & jnp.logical_not(keep), NEG, 0.0).astype(jnp.bfloat16)
        for h in range(HEADS):
            proj[1, h, head_dim:, :] = bias

        def part(j, carry):
            y = lax.dot_general(wt[j], x, NT, preferred_element_type=jnp.float32)
            proj[j, :, :head_dim, :] = y.astype(jnp.bfloat16).reshape(HEADS, head_dim, rows)
            return carry

        lax.fori_loop(0, 3, part, 0)

    local_pos = me * rows + lane

    def near(s, carry):
        project(x_near[s], local_pos < counts_ref[s])

        def head(h, carry):
            for b in range(nblocks):
                cols = slice(b * BLOCK, (b + 1) * BLOCK)
                out, lse = attend(
                    proj[1, h, :, cols], proj[0, h, :, cols], proj[2, h, :, cols], head_dim
                )
                near_out[s, h, :, cols] = out
                near_lse[s, h, :, cols] = lse
            return carry

        lax.fori_loop(0, HEADS, head, 0, unroll=4)
        return carry

    lax.fori_loop(0, slides, near, 0)

    class_pos = lane * ratio + me

    def far(s, carry):
        def arrive(k, carry):
            x_arrival(s, partner(k)).wait_recv()
            return carry

        lax.fori_loop(1, ratio, arrive, 0)
        x_recv[s, me] = x_send[s, me]
        project(x_recv[s].reshape(rows, width), class_pos < counts_ref[s])

        def head(h, carry):
            out, lse = attend(proj[1, h], proj[0, h], proj[2, h], head_dim)
            o_t[h] = out.astype(jnp.bfloat16)
            l_t[h] = lse
            return carry

        lax.fori_loop(0, HEADS, head, 0, unroll=2)
        o_send[s] = o_t[...].reshape(width, rows).T.reshape(ratio, chunk, width)
        lse = l_t[...].reshape(HEADS, rows)
        for d in range(ratio):
            l_send[s, d] = lse[:, d * chunk : (d + 1) * chunk]

        def send(k, carry):
            o_copy(s, partner(k), me).start()
            l_copy(s, partner(k), me).start()
            return carry

        lax.fori_loop(1, ratio, send, 0)
        return carry

    lax.fori_loop(0, slides, far, 0)

    def mix(s, carry):
        def arrive(k, carry):
            o_copy(s, partner(k), partner(k)).wait_recv()
            l_copy(s, partner(k), partner(k)).wait_recv()
            return carry

        lax.fori_loop(1, ratio, arrive, 0)
        o_recv[s, me] = o_send[s, me]
        l_recv[s, me] = l_send[s, me]
        for c in range(ratio):
            l_rows[c] = l_recv[s, c].T
        far_lse = jnp.dot(
            l_rows[...].reshape(rows, HEADS).T,
            spread_ref[...].astype(jnp.float32),
            precision=lax.Precision.HIGHEST,
            preferred_element_type=jnp.float32,
        ).reshape(HEADS, 1, rows)
        n_lse = near_lse[s]
        top = jnp.maximum(n_lse, far_lse)
        n_w = jnp.exp(n_lse - top)
        f_w = jnp.exp(far_lse - top)
        inv = 1.0 / (n_w + f_w)
        n_w = n_w * inv
        f_w = f_w * inv
        far_out = lax.dot_general(
            o_recv[s].reshape(rows, width),
            spread_ref[...],
            TN,
            preferred_element_type=jnp.float32,
        ).reshape(HEADS, head_dim, rows)
        mixed = (n_w * near_out[s] + f_w * far_out).astype(jnp.bfloat16)
        mixed_ref[...] = mixed.reshape(width, rows).T
        return carry

    def finish(s, carry):
        mix(s, carry)
        f32, bf16 = jnp.float32, jnp.bfloat16
        start = me * rows
        count = counts_ref[s]
        resid = tiles_ref[s].astype(f32) + jnp.dot(
            mixed_ref[...], wo_ref[...], preferred_element_type=f32
        )
        normed = normalize(resid, gain2_ref[...].reshape(1, width)).astype(bf16)
        ff = fi_ref.shape[1]
        step = width
        out = resid
        for j in range(0, ff, step):
            h = jnp.dot(normed, fi_ref[:, j : j + step], preferred_element_type=f32)
            act = gelu(h).astype(bf16)
            out = out + jnp.dot(act, fo_ref[j : j + step, :], preferred_element_type=f32)
        rowpos = start + lax.broadcasted_iota(jnp.int32, (rows, width), 0)
        encoded = jnp.where(rowpos < count, out, 0.0).astype(bf16)
        enc_ref[s] = encoded
        zed = jnp.dot(encoded, pw_ref[...], preferred_element_type=f32)
        hidden = zed.shape[1] // 2
        gate = jnp.tanh(zed[:, :hidden]) * jax.nn.sigmoid(zed[:, hidden:])
        logits = lax.dot_general(
            cw_ref[...], gate, NT, precision=lax.Precision.HIGHEST, preferred_element_type=f32
        )
        keep = start + lax.broadcasted_iota(jnp.int32, (classes, rows), 1) < count
        logits = jnp.where(keep, logits, NEG)

        peak = jnp.max(logits, axis=1, keepdims=True)
        expo = jnp.where(keep, jnp.exp(logits - peak), 0.0)
        numer = jnp.dot(
            expo, encoded.astype(f32), precision=lax.Precision.HIGHEST, preferred_element_type=f32
        )
        total = jnp.sum(expo, axis=1, keepdims=True)
        for c in range(classes):
            row = slice(c, c + 1)
            stat[s, c, :, :width] = numer[row]
            stat[s, c, :, width : width + 128] = jnp.broadcast_to(total[row], (1, 128))
            stat[s, c, :, width + 128 :] = jnp.broadcast_to(peak[row], (1, 128))

        def send(k, carry):
            @pl.when(partner(k) < classes)
            def _():
                s_copy(s, partner(k), me).start()

            return carry

        lax.fori_loop(1, ratio, send, 0)
        return carry

    for load in loads[1:]:
        load.wait()
    lax.fori_loop(0, slides, finish, 0)

    @pl.when(me < classes)
    def _():
        for s in range(slides):

            def arrive(k, carry, s=s):
                s_copy(s, me, partner(k)).wait_recv()
                return carry

            lax.fori_loop(1, ratio, arrive, 0)
            stat_recv[s, me] = stat[s, me]
            peaks = stat_recv[s, :, :, width + 128 :]
            fade = jnp.exp(peaks - jnp.max(peaks, axis=0, keepdims=True))
            inv = 1.0 / jnp.sum(stat_recv[s, :, :, width : width + 128] * fade, axis=0)
            for j in range(0, width, 128):
                numer = jnp.sum(stat_recv[s, :, :, j : j + 128] * fade, axis=0)
                row_send[s, :, j : j + 128] = numer * inv

        def send(k, carry):
            r_copy(partner(k), me).start()
            return carry

        lax.fori_loop(1, ratio, send, 0)
        row_recv[me] = row_send[...]

    def collect(k, carry):
        @pl.when(partner(k) < classes)
        def _():
            r_copy(partner(k), partner(k)).wait_recv()

        return carry

    lax.fori_loop(1, ratio, collect, 0)
    for c in range(classes):
        for s in range(slides):
            pooled_ref[s, c : c + 1, :] = row_recv[c, s]

    def drain(i, carry):
        s = i // (ratio - 1)
        peer = partner(i % (ratio - 1) + 1)
        x_copy(s, peer).wait_send()
        o_copy(s, peer, me).wait_send()
        l_copy(s, peer, me).wait_send()

        @pl.when(peer < classes)
        def _():
            s_copy(s, peer, me).wait_send()

        return carry

    lax.fori_loop(0, slides * (ratio - 1), drain, 0)

    @pl.when(me < classes)
    def _():
        def sent(k, carry):
            r_copy(partner(k), me).wait_send()
            return carry

        lax.fori_loop(1, ratio, sent, 0)


def layer(counts, tiles, gain, gain2, cw, w, wo, fi, fo, pw, ratio):
    slides, rows, width = tiles.shape
    head_dim = width // HEADS
    chunk = rows // ratio
    bf16, f32 = jnp.bfloat16, jnp.float32
    classes = cw.shape[0]
    vmem = pl.BlockSpec(memory_space=pltpu.VMEM)
    hbm = pl.BlockSpec(memory_space=pl.ANY)
    sem = pltpu.SemaphoreType.DMA((slides, ratio))
    return pl.pallas_call(
        functools.partial(layer_kernel, ratio),
        out_shape=(
            jax.ShapeDtypeStruct((slides, rows, width), bf16),
            jax.ShapeDtypeStruct((slides, classes, width), f32),
        ),
        in_specs=[pl.BlockSpec(memory_space=pltpu.SMEM), hbm, vmem, vmem, vmem] + [hbm] * 5,
        out_specs=(vmem, vmem),
        scratch_shapes=[
            pltpu.VMEM(tiles.shape, bf16),
            pltpu.VMEM(w.shape, bf16),
            pltpu.VMEM(wo.shape, bf16),
            pltpu.VMEM(fi.shape, bf16),
            pltpu.VMEM(fo.shape, bf16),
            pltpu.VMEM(pw.shape, bf16),
            pltpu.VMEM((3, width, width), bf16),
            pltpu.VMEM((rows, rows), bf16),
            pltpu.VMEM((slides, rows, width), bf16),
            pltpu.VMEM((slides, ratio, chunk, width), bf16),
            pltpu.VMEM((slides, ratio, chunk, width), bf16),
            pltpu.VMEM((3, HEADS, head_dim + AUG, rows), bf16),
            pltpu.VMEM((slides, HEADS, head_dim, rows), f32),
            pltpu.VMEM((slides, HEADS, 1, rows), f32),
            pltpu.VMEM((HEADS, head_dim, rows), bf16),
            pltpu.VMEM((HEADS, 1, rows), f32),
            pltpu.VMEM((slides, ratio, chunk, width), bf16),
            pltpu.VMEM((slides, ratio, chunk, width), bf16),
            pltpu.VMEM((slides, ratio, HEADS, chunk), f32),
            pltpu.VMEM((slides, ratio, HEADS, chunk), f32),
            pltpu.VMEM((ratio, chunk, HEADS), f32),
            pltpu.VMEM((rows, width), bf16),
            pltpu.VMEM((slides, classes, 1, width + 256), f32),
            pltpu.VMEM((slides, ratio, 1, width + 256), f32),
            pltpu.VMEM((slides, 1, width), f32),
            pltpu.VMEM((ratio, slides, 1, width), f32),
            sem,
            sem,
            sem,
            sem,
            sem,
            sem,
            sem,
            sem,
            pltpu.SemaphoreType.DMA((ratio,)),
            pltpu.SemaphoreType.DMA((ratio,)),
            pltpu.SemaphoreType.DMA((slides,)),
            pltpu.SemaphoreType.DMA((5,)),
        ],
        compiler_params=pltpu.CompilerParams(
            collective_id=0, has_side_effects=True, vmem_limit_bytes=60 * 2**20
        ),
        cost_estimate=pl.CostEstimate(
            flops=2 * slides * rows * width * width * 8,
            bytes_accessed=8 * slides * rows * width,
            transcendentals=0,
        ),
    )(counts, tiles, gain, gain2, cw, w, wo, fi, fo, pw)


def local(
    tiles,
    counts,
    ln1_gain,
    qkv_weight,
    out_weight,
    ln2_gain,
    ff_in,
    ff_out,
    pool_weight,
    class_weight,
):
    ratio = lax.axis_size("seq")
    pw = lax.all_gather(pool_weight, "grp", axis=0, tiled=True)
    return layer(
        counts,
        tiles,
        ln1_gain,
        ln2_gain,
        class_weight.T,
        qkv_weight,
        out_weight,
        ff_in,
        ff_out,
        pw,
        ratio,
    )


def solution(mesh):
    placed = (P("grp", "seq", None), P("grp"), P(), P(), P(), P(), P(), P(), P("grp", None), P())
    return jax.shard_map(
        local,
        mesh=mesh,
        in_specs=placed,
        out_specs=(P("grp", "seq", None), P("grp", None, None)),
        check_vma=False,
    )
```

```python
import functools
import math

import jax
import jax.numpy as jnp
from jax import lax
from jax.experimental import pallas as pl
from jax.experimental.pallas import tpu as pltpu
from jax.sharding import PartitionSpec as P

HEADS = 16
BLOCK = 256
AUG = 16
NEG = -1e30
NT = (((1,), (1,)), ((), ()))
TN = (((0,), (0,)), ((), ()))


def normalize(xf, gain):
    centre = jnp.mean(xf, axis=-1, keepdims=True)
    spread = jnp.mean((xf - centre) ** 2, axis=-1, keepdims=True)
    return (xf - centre) * lax.rsqrt(spread + 1e-05) * gain


def spread_matrix(rows, ratio):
    chunk = rows // ratio
    r = lax.broadcasted_iota(jnp.int32, (rows, rows), 0)
    t = lax.broadcasted_iota(jnp.int32, (rows, rows), 1)
    return jnp.where((r % chunk) * ratio + r // chunk == t, 1.0, 0.0)


def attend(kt, qt, vt, head_dim):
    scale = 1.0 / head_dim**0.5
    c = scale * math.log2(math.e)
    s = lax.dot_general(kt, qt, TN, preferred_element_type=jnp.float32)
    m = jnp.max(s, axis=0, keepdims=True)
    p = jnp.exp2((s - m) * c).astype(jnp.bfloat16)
    o = jnp.dot(vt, p, preferred_element_type=jnp.float32)
    total = o[head_dim : head_dim + 1]
    return o[:head_dim] / total, m * scale + jnp.log(total)


def gelu(x):
    return 0.5 * x * (1.0 + lax.erf(x * math.sqrt(0.5)))


def layer_kernel(
    ratio,
    counts_ref,
    tiles_hbm,
    gain_ref,
    gain2_ref,
    cw_ref,
    w_hbm,
    wo_hbm,
    fi_hbm,
    fo_hbm,
    pw_hbm,
    enc_ref,
    pooled_ref,
    tiles_ref,
    w_ref,
    wo_ref,
    fi_ref,
    fo_ref,
    pw_ref,
    wt,
    spread_ref,
    x_near,
    x_send,
    x_recv,
    proj,
    near_out,
    near_lse,
    o_t,
    l_t,
    o_send,
    o_recv,
    l_send,
    l_recv,
    l_rows,
    mixed_ref,
    stat,
    stat_recv,
    row_send,
    row_recv,
    x_ss,
    x_rs,
    o_ss,
    o_rs,
    l_ss,
    l_rs,
    s_ss,
    s_rs,
    r_ss,
    r_rs,
    t_sem,
    w_sem,
    pw_ss,
    pw_rs,
):
    me = lax.axis_index("seq")
    part_me = lax.axis_index("grp")
    parts = pw_ref.shape[0]
    slides, rows, width = tiles_ref.shape
    head_dim = width // HEADS
    nblocks = rows // BLOCK
    chunk = rows // ratio
    classes = cw_ref.shape[0]
    tile_loads = [
        pltpu.make_async_copy(tiles_hbm.at[s], tiles_ref.at[s], t_sem.at[s]) for s in range(slides)
    ]
    pairs = (
        (w_hbm, w_ref),
        (wo_hbm, wo_ref),
        (fi_hbm, fi_ref),
        (fo_hbm, fo_ref),
        (pw_hbm, pw_ref.at[part_me]),
    )
    loads = [pltpu.make_async_copy(a, b, w_sem.at[i]) for i, (a, b) in enumerate(pairs)]
    for load in tile_loads + loads:
        load.start()

    def x_copy(s, peer):
        return pltpu.make_async_remote_copy(
            src_ref=x_send.at[s, peer],
            dst_ref=x_recv.at[s, me],
            send_sem=x_ss.at[s, peer],
            recv_sem=x_rs.at[s, me],
            device_id={"seq": peer},
            device_id_type=pl.DeviceIdType.MESH,
        )

    def x_arrival(s, peer):
        return pltpu.make_async_remote_copy(
            src_ref=x_send.at[s, peer],
            dst_ref=x_recv.at[s, peer],
            send_sem=x_ss.at[s, peer],
            recv_sem=x_rs.at[s, peer],
            device_id={"seq": peer},
            device_id_type=pl.DeviceIdType.MESH,
        )

    def o_copy(s, peer, slot):
        return pltpu.make_async_remote_copy(
            src_ref=o_send.at[s, peer],
            dst_ref=o_recv.at[s, slot],
            send_sem=o_ss.at[s, peer],
            recv_sem=o_rs.at[s, slot],
            device_id={"seq": peer},
            device_id_type=pl.DeviceIdType.MESH,
        )

    def l_copy(s, peer, slot):
        return pltpu.make_async_remote_copy(
            src_ref=l_send.at[s, peer],
            dst_ref=l_recv.at[s, slot],
            send_sem=l_ss.at[s, peer],
            recv_sem=l_rs.at[s, slot],
            device_id={"seq": peer},
            device_id_type=pl.DeviceIdType.MESH,
        )

    def s_copy(s, owner, slot):
        return pltpu.make_async_remote_copy(
            src_ref=stat.at[s, owner],
            dst_ref=stat_recv.at[s, slot],
            send_sem=s_ss.at[s, owner],
            recv_sem=s_rs.at[s, slot],
            device_id={"seq": owner},
            device_id_type=pl.DeviceIdType.MESH,
        )

    def r_copy(peer, slot):
        return pltpu.make_async_remote_copy(
            src_ref=row_send,
            dst_ref=row_recv.at[slot],
            send_sem=r_ss.at[peer],
            recv_sem=r_rs.at[slot],
            device_id={"seq": peer},
            device_id_type=pl.DeviceIdType.MESH,
        )

    def partner(k):
        return lax.rem(me + k, ratio)

    def part_partner(k):
        return lax.rem(part_me + k, parts)

    def w_copy(peer, slot):
        return pltpu.make_async_remote_copy(
            src_ref=pw_hbm,
            dst_ref=pw_ref.at[slot],
            send_sem=pw_ss.at[peer],
            recv_sem=pw_rs.at[slot],
            device_id={"grp": peer},
            device_id_type=pl.DeviceIdType.MESH,
        )

    barrier = pltpu.get_barrier_semaphore()
    for k in range(1, ratio):
        pl.semaphore_signal(
            barrier, inc=1, device_id={"seq": partner(k)}, device_id_type=pl.DeviceIdType.MESH
        )
    for k in range(1, parts):
        pl.semaphore_signal(
            barrier, inc=1, device_id={"grp": part_partner(k)}, device_id_type=pl.DeviceIdType.MESH
        )

    spread_ref[...] = spread_matrix(rows, ratio).astype(jnp.bfloat16)
    for s in range(slides):
        tile_loads[s].wait()
        xf = tiles_ref[s].astype(jnp.float32)
        normed = normalize(xf, gain_ref[...].reshape(1, width)).astype(jnp.bfloat16)
        x_near[s] = normed
        moved = jnp.dot(spread_ref[...], normed, preferred_element_type=jnp.float32)
        x_send[s] = moved.astype(jnp.bfloat16).reshape(ratio, chunk, width)
        if s == 0:
            pl.semaphore_wait(barrier, ratio - 1 + parts - 1)

        def send(k, carry, s=s):
            x_copy(s, partner(k)).start()
            return carry

        lax.fori_loop(1, ratio, send, 0)

    for k in range(1, parts):
        w_copy(part_partner(k), part_me).start()

    loads[0].wait()
    for j in range(3):
        wt[j] = w_ref[:, j * width : (j + 1) * width].T
    first = lax.broadcasted_iota(jnp.int32, (AUG, rows), 0) == 0
    lane = lax.broadcasted_iota(jnp.int32, (AUG, rows), 1)
    ones = jnp.where(first, 1.0, 0.0).astype(jnp.bfloat16)
    for h in range(HEADS):
        proj[0, h, head_dim:, :] = ones
        proj[2, h, head_dim:, :] = ones

    def project(x, keep):
        bias = jnp.where(first & jnp.logical_not(keep), NEG, 0.0).astype(jnp.bfloat16)
        for h in range(HEADS):
            proj[1, h, head_dim:, :] = bias

        def part(j, carry):
            y = lax.dot_general(wt[j], x, NT, preferred_element_type=jnp.float32)
            proj[j, :, :head_dim, :] = y.astype(jnp.bfloat16).reshape(HEADS, head_dim, rows)
            return carry

        lax.fori_loop(0, 3, part, 0)

    local_pos = me * rows + lane

    def near(s, carry):
        project(x_near[s], local_pos < counts_ref[s])

        def head(h, carry):
            for b in range(nblocks):
                cols = slice(b * BLOCK, (b + 1) * BLOCK)
                out, lse = attend(
                    proj[1, h, :, cols], proj[0, h, :, cols], proj[2, h, :, cols], head_dim
                )
                near_out[s, h, :, cols] = out
                near_lse[s, h, :, cols] = lse
            return carry

        lax.fori_loop(0, HEADS, head, 0, unroll=4)
        return carry

    near(0, 0)

    class_pos = lane * ratio + me

    def far(s, carry):
        def arrive(k, carry):
            x_arrival(s, partner(k)).wait_recv()
            return carry

        lax.fori_loop(1, ratio, arrive, 0)
        x_recv[s, me] = x_send[s, me]
        project(x_recv[s].reshape(rows, width), class_pos < counts_ref[s])

        def head(h, carry):
            out, lse = attend(proj[1, h], proj[0, h], proj[2, h], head_dim)
            o_t[h] = out.astype(jnp.bfloat16)
            l_t[h] = lse
            return carry

        lax.fori_loop(0, HEADS, head, 0, unroll=2)
        o_send[s] = o_t[...].reshape(width, rows).T.reshape(ratio, chunk, width)
        lse = l_t[...].reshape(HEADS, rows)
        for d in range(ratio):
            l_send[s, d] = lse[:, d * chunk : (d + 1) * chunk]

        def send(k, carry):
            o_copy(s, partner(k), me).start()
            l_copy(s, partner(k), me).start()
            return carry

        lax.fori_loop(1, ratio, send, 0)
        return carry

    lax.fori_loop(0, slides, far, 0)
    lax.fori_loop(1, slides, near, 0)

    def mix(s, carry):
        def arrive(k, carry):
            o_copy(s, partner(k), partner(k)).wait_recv()
            l_copy(s, partner(k), partner(k)).wait_recv()
            return carry

        lax.fori_loop(1, ratio, arrive, 0)
        o_recv[s, me] = o_send[s, me]
        l_recv[s, me] = l_send[s, me]
        for c in range(ratio):
            l_rows[c] = l_recv[s, c].T
        far_lse = jnp.dot(
            l_rows[...].reshape(rows, HEADS).T,
            spread_ref[...].astype(jnp.float32),
            precision=lax.Precision.HIGHEST,
            preferred_element_type=jnp.float32,
        ).reshape(HEADS, 1, rows)
        n_lse = near_lse[s]
        top = jnp.maximum(n_lse, far_lse)
        n_w = jnp.exp(n_lse - top)
        f_w = jnp.exp(far_lse - top)
        inv = 1.0 / (n_w + f_w)
        n_w = n_w * inv
        f_w = f_w * inv
        far_out = lax.dot_general(
            o_recv[s].reshape(rows, width),
            spread_ref[...],
            TN,
            preferred_element_type=jnp.float32,
        ).reshape(HEADS, head_dim, rows)
        mixed = (n_w * near_out[s] + f_w * far_out).astype(jnp.bfloat16)
        mixed_ref[...] = mixed.reshape(width, rows).T
        return carry

    def finish(s, carry):
        mix(s, carry)
        f32, bf16 = jnp.float32, jnp.bfloat16
        start = me * rows
        count = counts_ref[s]
        resid = tiles_ref[s].astype(f32) + jnp.dot(
            mixed_ref[...], wo_ref[...], preferred_element_type=f32
        )
        normed = normalize(resid, gain2_ref[...].reshape(1, width)).astype(bf16)
        ff = fi_ref.shape[1]
        step = width
        out = resid
        for j in range(0, ff, step):
            h = jnp.dot(normed, fi_ref[:, j : j + step], preferred_element_type=f32)
            act = gelu(h).astype(bf16)
            out = out + jnp.dot(act, fo_ref[j : j + step, :], preferred_element_type=f32)
        rowpos = start + lax.broadcasted_iota(jnp.int32, (rows, width), 0)
        encoded = jnp.where(rowpos < count, out, 0.0).astype(bf16)
        enc_ref[s] = encoded
        zed = jnp.dot(encoded, pw_ref[...].reshape(width, -1), preferred_element_type=f32)
        hidden = zed.shape[1] // 2
        gate = jnp.tanh(zed[:, :hidden]) * jax.nn.sigmoid(zed[:, hidden:])
        logits = lax.dot_general(
            cw_ref[...], gate, NT, precision=lax.Precision.HIGHEST, preferred_element_type=f32
        )
        keep = start + lax.broadcasted_iota(jnp.int32, (classes, rows), 1) < count
        logits = jnp.where(keep, logits, NEG)

        peak = jnp.max(logits, axis=1, keepdims=True)
        expo = jnp.where(keep, jnp.exp(logits - peak), 0.0)
        numer = jnp.dot(
            expo, encoded.astype(f32), precision=lax.Precision.HIGHEST, preferred_element_type=f32
        )
        total = jnp.sum(expo, axis=1, keepdims=True)
        for c in range(classes):
            row = slice(c, c + 1)
            stat[s, c, :, :width] = numer[row]
            stat[s, c, :, width : width + 128] = jnp.broadcast_to(total[row], (1, 128))
            stat[s, c, :, width + 128 :] = jnp.broadcast_to(peak[row], (1, 128))

        def send(k, carry):
            @pl.when(partner(k) < classes)
            def _():
                s_copy(s, partner(k), me).start()

            return carry

        lax.fori_loop(1, ratio, send, 0)
        return carry

    for load in loads[1:]:
        load.wait()
    for k in range(1, parts):
        w_copy(part_partner(k), part_partner(k)).wait_recv()
    lax.fori_loop(0, slides, finish, 0)

    @pl.when(me < classes)
    def _():
        for s in range(slides):

            def arrive(k, carry, s=s):
                s_copy(s, me, partner(k)).wait_recv()
                return carry

            lax.fori_loop(1, ratio, arrive, 0)
            stat_recv[s, me] = stat[s, me]
            peaks = stat_recv[s, :, :, width + 128 :]
            fade = jnp.exp(peaks - jnp.max(peaks, axis=0, keepdims=True))
            inv = 1.0 / jnp.sum(stat_recv[s, :, :, width : width + 128] * fade, axis=0)
            for j in range(0, width, 128):
                numer = jnp.sum(stat_recv[s, :, :, j : j + 128] * fade, axis=0)
                row_send[s, :, j : j + 128] = numer * inv

        def send(k, carry):
            r_copy(partner(k), me).start()
            return carry

        lax.fori_loop(1, ratio, send, 0)
        row_recv[me] = row_send[...]

    def collect(k, carry):
        @pl.when(partner(k) < classes)
        def _():
            r_copy(partner(k), partner(k)).wait_recv()

        return carry

    lax.fori_loop(1, ratio, collect, 0)
    for c in range(classes):
        for s in range(slides):
            pooled_ref[s, c : c + 1, :] = row_recv[c, s]

    def drain(i, carry):
        s = i // (ratio - 1)
        peer = partner(i % (ratio - 1) + 1)
        x_copy(s, peer).wait_send()
        o_copy(s, peer, me).wait_send()
        l_copy(s, peer, me).wait_send()

        @pl.when(peer < classes)
        def _():
            s_copy(s, peer, me).wait_send()

        return carry

    lax.fori_loop(0, slides * (ratio - 1), drain, 0)
    for k in range(1, parts):
        w_copy(part_partner(k), part_me).wait_send()

    @pl.when(me < classes)
    def _():
        def sent(k, carry):
            r_copy(partner(k), me).wait_send()
            return carry

        lax.fori_loop(1, ratio, sent, 0)


def layer(counts, tiles, gain, gain2, cw, w, wo, fi, fo, pw, ratio):
    slides, rows, width = tiles.shape
    head_dim = width // HEADS
    chunk = rows // ratio
    bf16, f32 = jnp.bfloat16, jnp.float32
    classes = cw.shape[0]
    parts = lax.axis_size("grp")
    vmem = pl.BlockSpec(memory_space=pltpu.VMEM)
    hbm = pl.BlockSpec(memory_space=pl.ANY)
    sem = pltpu.SemaphoreType.DMA((slides, ratio))
    return pl.pallas_call(
        functools.partial(layer_kernel, ratio),
        out_shape=(
            jax.ShapeDtypeStruct((slides, rows, width), bf16),
            jax.ShapeDtypeStruct((slides, classes, width), f32),
        ),
        in_specs=[pl.BlockSpec(memory_space=pltpu.SMEM), hbm, vmem, vmem, vmem] + [hbm] * 5,
        out_specs=(vmem, vmem),
        scratch_shapes=[
            pltpu.VMEM(tiles.shape, bf16),
            pltpu.VMEM(w.shape, bf16),
            pltpu.VMEM(wo.shape, bf16),
            pltpu.VMEM(fi.shape, bf16),
            pltpu.VMEM(fo.shape, bf16),
            pltpu.VMEM((parts,) + pw.shape, bf16),
            pltpu.VMEM((3, width, width), bf16),
            pltpu.VMEM((rows, rows), bf16),
            pltpu.VMEM((slides, rows, width), bf16),
            pltpu.VMEM((slides, ratio, chunk, width), bf16),
            pltpu.VMEM((slides, ratio, chunk, width), bf16),
            pltpu.VMEM((3, HEADS, head_dim + AUG, rows), bf16),
            pltpu.VMEM((slides, HEADS, head_dim, rows), f32),
            pltpu.VMEM((slides, HEADS, 1, rows), f32),
            pltpu.VMEM((HEADS, head_dim, rows), bf16),
            pltpu.VMEM((HEADS, 1, rows), f32),
            pltpu.VMEM((slides, ratio, chunk, width), bf16),
            pltpu.VMEM((slides, ratio, chunk, width), bf16),
            pltpu.VMEM((slides, ratio, HEADS, chunk), f32),
            pltpu.VMEM((slides, ratio, HEADS, chunk), f32),
            pltpu.VMEM((ratio, chunk, HEADS), f32),
            pltpu.VMEM((rows, width), bf16),
            pltpu.VMEM((slides, classes, 1, width + 256), f32),
            pltpu.VMEM((slides, ratio, 1, width + 256), f32),
            pltpu.VMEM((slides, 1, width), f32),
            pltpu.VMEM((ratio, slides, 1, width), f32),
            sem,
            sem,
            sem,
            sem,
            sem,
            sem,
            sem,
            sem,
            pltpu.SemaphoreType.DMA((ratio,)),
            pltpu.SemaphoreType.DMA((ratio,)),
            pltpu.SemaphoreType.DMA((slides,)),
            pltpu.SemaphoreType.DMA((5,)),
            pltpu.SemaphoreType.DMA((parts,)),
            pltpu.SemaphoreType.DMA((parts,)),
        ],
        compiler_params=pltpu.CompilerParams(
            collective_id=0, has_side_effects=True, vmem_limit_bytes=48 * 2**20
        ),
        cost_estimate=pl.CostEstimate(
            flops=2 * slides * rows * width * width * 8,
            bytes_accessed=8 * slides * rows * width,
            transcendentals=0,
        ),
    )(counts, tiles, gain, gain2, cw, w, wo, fi, fo, pw)


def local(
    tiles,
    counts,
    ln1_gain,
    qkv_weight,
    out_weight,
    ln2_gain,
    ff_in,
    ff_out,
    pool_weight,
    class_weight,
):
    ratio = lax.axis_size("seq")
    return layer(
        counts,
        tiles,
        ln1_gain,
        ln2_gain,
        class_weight.T,
        qkv_weight,
        out_weight,
        ff_in,
        ff_out,
        pool_weight,
        ratio,
    )


def solution(mesh):
    placed = (P("grp", "seq", None), P("grp"), P(), P(), P(), P(), P(), P(), P("grp", None), P())
    return jax.shard_map(
        local,
        mesh=mesh,
        in_specs=placed,
        out_specs=(P("grp", "seq", None), P("grp", None, None)),
        check_vma=False,
    )
```
